256 devices in a mesh: row: 16 (over y, x_hi, core), col: 16 (over z, x_lo).
Axes of the slice: x: 4 (x_hi: 2, x_lo: 2; x = x_hi * 2 + x_lo), y: 4, z: 8, core: 2. Of those that a mesh axis runs over, the one named last changes fastest.
Arguments:
- integrals: bfloat16 [24576, 1536], P('row', 'col'), may hold values from -0.15625 to 0.15625
- amplitudes: bfloat16 [1536, 24576], P('row', 'col'), may hold values from -6 to 6
- energies: float32 [24576], replicated, may hold values from 0.5 to 4
Outputs:
- residual: float32 [24576, 24576], P('row', 'col')
The draws below stay inside these ranges and needn't reach their ends.
All inputs are finite; a program needn't handle non-finite values.
Results may differ from the reference program's by a relative error of at most 0.0021.
Values may be sent and summed in bfloat16 or wider, within the bound.
A program may use at most 128 MiB of HBM per device.

```python
import math
import jax
import jax.numpy as jnp

NPAIR = 24576
KPAIR = 1536


def steps_of(own_key, dims, pieces, smallest, high):
    def one(position, blocks):
        steps = jax.random.uniform(jax.random.fold_in(jax.random.fold_in(own_key, 6), position), (blocks,), jnp.float32, smallest / len(pieces), high / len(pieces))
        return jnp.repeat(jnp.exp(steps), dims[position] // blocks).reshape((-1,) + (1,) * (len(dims) - position - 1))

    loudness = one(*pieces[0])
    for cut in pieces[1:]:
        loudness = loudness * one(*cut)
    return loudness


def scatter_about(key, dims, width, bound, split=(), dtype=jnp.bfloat16):
    loudness = steps_of(key, dims, split, -0.22, 0.18) if split else 1.0
    values = jax.random.normal(key, dims, jnp.float32) * width * loudness
    return jnp.minimum(jnp.maximum(values, -bound), bound).astype(dtype)


def setup_inputs(seed: int = 0) -> dict:
    splits = jax.random.split(jax.random.key(seed), 4)
    return {
        "integrals": scatter_about(splits[0], (NPAIR, KPAIR), KPAIR ** -0.5, 0.15625, ((0, 16), (1, 16))),
        "amplitudes": scatter_about(splits[1], (KPAIR, NPAIR), 1.0, 6.0, ((0, 16), (1, 16))),
        "energies": jnp.clip(jnp.exp(jax.random.uniform(splits[2], (NPAIR,), jnp.float32, math.log(0.5), math.log(4.0))), 0.5, 4.0),
    }


def reference(integrals, amplitudes, energies):
    ladder = jnp.dot(integrals, amplitudes, preferred_element_type=jnp.float32)
    ladder_half = ladder.astype(jnp.bfloat16)
    denom = energies[:, None] + energies[None, :]
    return (ladder + ladder_half.T.astype(jnp.float32)) / denom
```

```python
import functools

import jax
import jax.numpy as jnp
from jax import lax
from jax.experimental import pallas as pl
from jax.experimental.pallas import tpu as pltpu
from jax.sharding import PartitionSpec as P

MESH = pl.DeviceIdType.MESH
N_SEND = 96
N_RECV = 64
MIB = 1 << 20


def gather_kernel(i_ref, a_ref, out_ref, rows, cols, acc, send_sems, recv_sems):
    r, c = lax.axis_index("row"), lax.axis_index("col")
    x_lo, x_hi, core = lax.rem(c, 2), lax.rem(r // 2, 2), lax.rem(r, 2)
    z = c // 2
    to_x = (r, c + 1 - 2 * x_lo)
    to_zp, to_zm = (r, lax.rem(c + 2, 16)), (r, lax.rem(c + 14, 16))
    to_h = (r + 2 - 4 * x_hi, c)
    to_yp, to_ym = (lax.rem(r + 4, 16), c), (lax.rem(r + 12, 16), c)
    to_core = (r + 1 - 2 * core, c)
    to_t = (c, r)

    sends, recv_ids = [], {}

    def recv_id(key):
        return recv_ids.setdefault(key, len(recv_ids))

    def copy(panel, t, slot, device, key, src=None):
        return pltpu.make_async_remote_copy(
            src_ref=panel.at[t, slot] if src is None else src,
            dst_ref=panel.at[t, slot],
            send_sem=send_sems.at[len(sends)],
            recv_sem=recv_sems.at[recv_id(key)],
            device_id=device,
            device_id_type=MESH,
        )

    def send(*args, **kw):
        op = copy(*args, **kw)
        op.start()
        sends.append(op)

    def arrived(panel, t, slot, key):
        pltpu.make_async_remote_copy(
            src_ref=panel.at[t, slot], dst_ref=panel.at[t, slot],
            send_sem=send_sems.at[0], recv_sem=recv_sems.at[recv_id(key)],
            device_id=to_x, device_id_type=MESH,
        ).wait_recv()

    def rslot(d, own):
        j = lax.rem(c + 2 * d + 16, 16)
        return j if own else j + 1 - 2 * x_lo

    def cslot(d, own_h, own_core):
        i = lax.rem(r + 4 * d + 16, 16)
        i = i if own_h else i + 2 - 4 * x_hi
        return i if own_core else i + 1 - 2 * core

    reach_z = {0: (4, 3), 1: (3, 4)}
    reach_y = {0: (2, 1), 1: (1, 2)}

    def zsend(t, d, own, sign):
        if abs(d) < reach_z[t][0 if sign > 0 else 1]:
            here = rslot(d, own)
            send(rows, t, here, to_zp if sign > 0 else to_zm, ("z", t, sign, abs(d) + 1, own))

    def zwait(t, d, own, sign):
        arrived(rows, t, rslot(-sign * d, own), ("z", t, sign, d, own))

    def ysend(t, d, own_h, sign):
        if abs(d) < reach_y[t][0 if sign > 0 else 1]:
            send(cols, t, cslot(d, own_h, True), to_yp if sign > 0 else to_ym, ("y", t, sign, abs(d) + 1, own_h))

    def ywait(t, d, own_h, sign):
        arrived(cols, t, cslot(-sign * d, own_h, True), ("y", t, sign, d, own_h))

    def coresend(t, d, own_h):
        send(cols, t, cslot(d, own_h, True), to_core, ("core", t, d, own_h))

    def corewait(t, d, own_h):
        arrived(cols, t, cslot(d, own_h, False), ("core", t, d, own_h))

    def xsend(t, d):
        send(rows, t, rslot(d, True), to_x, ("x", t, d))

    def xwait(t, d):
        arrived(rows, t, rslot(d, False), ("x", t, d))

    def ystep(t, d, own_h, sign):
        ywait(t, d, own_h, sign)
        ysend(t, -sign * d, own_h, sign)
        coresend(t, -sign * d, own_h)

    def zstep(t, d, own, sign, across):
        zwait(t, d, own, sign)
        zsend(t, -sign * d, own, sign)
        if across:
            xsend(t, -sign * d)

    def cstart(t):
        send(cols, t, cslot(0, True, True), to_h, ("h", t))
        ysend(t, 0, True, 1)
        ysend(t, 0, True, -1)
        coresend(t, 0, True)

    def chi(t):
        arrived(cols, t, cslot(0, False, True), ("h", t))
        ysend(t, 0, False, 1)
        ysend(t, 0, False, -1)
        coresend(t, 0, False)

    def cores(t):
        lo, hi = (-2, 1) if t == 0 else (-1, 2)
        for d in range(lo, hi + 1):
            for own_h in (True, False):
                corewait(t, d, own_h)

    tile = 256
    target = {0: out_ref, 1: acc}

    def product(t, ds, first=False):
        blocks = [2 * lax.rem(z + d + 8, 8) for d in ds]
        dest = target[t]

        @pl.loop(0, 1536 // tile)
        def _(m):
            span = pl.ds(pl.multiple_of(m * tile, tile), tile)
            total = None
            for b in blocks:
                left = rows[t, pl.ds(b, 2), :, span].reshape(192, tile)
                right = cols[t, pl.ds(b, 2)].reshape(192, 1536)
                term = lax.dot_general(left, right, (((0,), (0,)), ((), ())), preferred_element_type=jnp.float32)
                total = term if total is None else total + term
            dest[span, :] = total if first else dest[span, :] + total

    barrier = pltpu.get_barrier_semaphore()
    for device in (to_x, to_zp, to_zm, to_h, to_yp, to_ym, to_core):
        pl.semaphore_signal(barrier, inc=1, device_id=device, device_id_type=MESH)

    @pl.when(r != c)
    def _():
        pl.semaphore_signal(barrier, inc=1, device_id=to_t, device_id_type=MESH)

    rows[0, c] = i_ref[...].T
    cols[0, r] = a_ref[...]

    @pl.when(r != c)
    def _():
        pl.semaphore_wait(barrier, 8)

    @pl.when(r == c)
    def _():
        pl.semaphore_wait(barrier, 7)

    t_a = pltpu.make_async_remote_copy(
        src_ref=cols.at[0, r], dst_ref=rows.at[1, r],
        send_sem=send_sems.at[N_SEND - 1], recv_sem=recv_sems.at[N_RECV - 1], device_id=to_t, device_id_type=MESH,
    )
    t_i = pltpu.make_async_remote_copy(
        src_ref=rows.at[0, c], dst_ref=cols.at[1, c],
        send_sem=send_sems.at[N_SEND - 2], recv_sem=recv_sems.at[N_RECV - 2], device_id=to_t, device_id_type=MESH,
    )

    @pl.when(r != c)
    def _():
        t_a.start()
        t_i.start()

    @pl.when(r == c)
    def _():
        rows[1, c] = a_ref[...]
        cols[1, r] = rows[0, c]

    zsend(0, 0, True, 1)
    zsend(0, 0, True, -1)
    xsend(0, 0)
    cstart(0)
    xwait(0, 0)
    zsend(0, 0, False, 1)
    zsend(0, 0, False, -1)
    chi(0)

    @pl.when(r != c)
    def _():
        t_a.wait_recv()

    zsend(1, 0, True, 1)
    zsend(1, 0, True, -1)
    xsend(1, 0)

    @pl.when(r != c)
    def _():
        t_i.wait_recv()

    cstart(1)
    for sign in (1, -1):
        zstep(0, 1, True, sign, False)
    for sign in (1, -1):
        ystep(0, 1, True, sign)
    chi(1)
    for sign in (1, -1):
        zstep(0, 1, False, sign, False)
    for sign in (1, -1):
        ystep(0, 1, False, sign)
    for sign in (1, -1):
        zstep(1, 1, True, sign, True)
    for own_h in (True, False):
        for sign in (1, -1):
            ystep(1, 1, own_h, sign)
    for own_h in (True, False):
        ystep(0, 2, own_h, 1)
    cores(0)
    product(0, (0,), True)
    for own in (True, False):
        for sign in (1, -1):
            zstep(0, 2, own, sign, False)
    for own_h in (True, False):
        ystep(1, 2, own_h, -1)
    for sign in (1, -1):
        zstep(1, 2, True, sign, True)
    product(0, (1, -1))
    cores(1)
    xwait(1, 0)
    product(1, (0,), True)
    for own in (True, False):
        for sign in (1, -1):
            zstep(0, 3, own, sign, False)
    for sign in (1, -1):
        zstep(1, 3, True, sign, True)
    product(0, (2, -2))
    for sign in (1, -1):
        xwait(1, -sign)
    product(1, (1, -1))
    for own in (True, False):
        zstep(0, 4, own, 1, False)
    zstep(1, 4, True, -1, True)
    product(0, (3, -3))
    for sign in (1, -1):
        xwait(1, -2 * sign)
    product(1, (2, -2))
    product(0, (-4,))
    for sign in (1, -1):
        xwait(1, -3 * sign)
    product(1, (3, -3))
    xwait(1, 4)
    last = 2 * lax.rem(z + 4, 8)

    @pl.loop(0, 1536 // tile)
    def _(m):
        span = pl.ds(pl.multiple_of(m * tile, tile), tile)
        left = rows[1, pl.ds(last, 2), :, span].reshape(192, tile)
        right = cols[1, pl.ds(last, 2)].reshape(192, 1536)
        term = lax.dot_general(left, right, (((0,), (0,)), ((), ())), preferred_element_type=jnp.float32)
        half = (acc[span, :] + term).astype(jnp.bfloat16)
        out_ref[span, :] = out_ref[span, :] + half.astype(jnp.float32)

    for op in sends:
        op.wait_send()

    @pl.when(r != c)
    def _():
        t_a.wait_send()
        t_i.wait_send()


def scale_kernel(sum_ref, row_e_ref, col_e_ref, out_ref, buffer, sems):
    tile = buffer.shape[1]
    steps = sum_ref.shape[0] // tile

    def put(m, slot):
        return pltpu.make_async_copy(
            buffer.at[slot], out_ref.at[pl.ds(pl.multiple_of(m * tile, tile), tile), :], sems.at[slot])

    @pl.loop(0, steps)
    def _(m):
        slot = lax.rem(m, 2)

        @pl.when(m >= 2)
        def _():
            put(m - 2, slot).wait()

        span = pl.ds(pl.multiple_of(m * tile, tile), tile)
        buffer[slot] = sum_ref[span, :] / (row_e_ref[span, :] + col_e_ref[...])
        put(m, slot).start()

    put(steps - 2, (steps - 2) % 2).wait()
    put(steps - 1, (steps - 1) % 2).wait()


def body(integrals, amplitudes, energies):
    size = integrals.shape[0]
    depth = amplitudes.shape[0]
    n = lax.axis_size("col")
    summed = pl.pallas_call(
        gather_kernel,
        out_shape=jax.ShapeDtypeStruct((size, size), jnp.float32),
        in_specs=[pl.BlockSpec(memory_space=pltpu.VMEM)] * 2,
        out_specs=pl.BlockSpec(memory_space=pltpu.VMEM),
        scratch_shapes=[
            pltpu.VMEM((2, n, depth, size), jnp.bfloat16),
            pltpu.VMEM((2, n, depth, size), jnp.bfloat16),
            pltpu.VMEM((size, size), jnp.float32),
            pltpu.SemaphoreType.DMA((N_SEND,)),
            pltpu.SemaphoreType.DMA((N_RECV,)),
        ],
        compiler_params=pltpu.CompilerParams(
            collective_id=0, has_side_effects=True, vmem_limit_bytes=44 * MIB),
    )(integrals, amplitudes)
    row_e = lax.dynamic_slice_in_dim(energies, lax.axis_index("row") * size, size, 0)[:, None]
    col_e = lax.dynamic_slice_in_dim(energies, lax.axis_index("col") * size, size, 0)[None, :]
    return pl.pallas_call(
        scale_kernel,
        out_shape=jax.ShapeDtypeStruct((size, size), jnp.float32),
        in_specs=[pl.BlockSpec(memory_space=pltpu.VMEM)] * 3,
        out_specs=pl.BlockSpec(memory_space=pl.ANY),
        scratch_shapes=[
            pltpu.VMEM((2, 128, size), jnp.float32),
            pltpu.SemaphoreType.DMA((2,)),
        ],
        compiler_params=pltpu.CompilerParams(vmem_limit_bytes=16 * MIB),
    )(summed, row_e, col_e)


def solution(mesh):
    return jax.shard_map(
        body,
        mesh=mesh,
        in_specs=(P("row", "col"), P("row", "col"), P()),
        out_specs=P("row", "col"),
        check_vma=False,
    )
```

```python
import functools

import jax
import jax.numpy as jnp
from jax import lax
from jax.experimental import pallas as pl
from jax.experimental.pallas import tpu as pltpu
from jax.sharding import PartitionSpec as P

MESH = pl.DeviceIdType.MESH
N_SEND = 192
N_RECV = 128
MIB = 1 << 20
PIECE = 384


def gather_kernel(i_ref, a_ref, out_ref, rows, cols, acc, stage_y, stage_z, load_sems, send_sems, recv_sems):
    r, c = lax.axis_index("row"), lax.axis_index("col")
    x_lo, x_hi, core = lax.rem(c, 2), lax.rem(r // 2, 2), lax.rem(r, 2)
    z, y = c // 2, r // 4
    to_x = (r, c + 1 - 2 * x_lo)
    to_zp, to_zm = (r, lax.rem(c + 2, 16)), (r, lax.rem(c + 14, 16))
    to_h = (r + 2 - 4 * x_hi, c)
    to_yp, to_ym = (lax.rem(r + 4, 16), c), (lax.rem(r + 12, 16), c)
    to_y2 = (lax.rem(r + 8, 16), c)
    to_core = (r + 1 - 2 * core, c)
    relay = x_hi == lax.rem(z, 2)
    at_home = relay & (core == x_lo)

    send_ids, recv_ids, plain = {}, {}, []

    def ids(table, key, count=1):
        if key not in table:
            table[key] = sum(n for _, n in table.values()), count
        return table[key][0]

    def copy(src, dst, device, send, recv):
        return pltpu.make_async_remote_copy(
            src_ref=src, dst_ref=dst, send_sem=send_sems.at[send], recv_sem=recv_sems.at[recv],
            device_id=device, device_id_type=MESH)

    def start(src, dst, device, key):
        op = copy(src, dst, device, ids(send_ids, key), ids(recv_ids, key))
        op.start()
        plain.append(op)

    def wait_at(dst, recv):
        copy(dst, dst, to_x, 0, recv).wait_recv()

    def arrived(dst, key):
        wait_at(dst, ids(recv_ids, key))

    def rslot(d, own):
        j = lax.rem(c + 2 * d + 16, 16)
        return j if own else j + 1 - 2 * lax.rem(j, 2)

    def cslot(d, own_h, own_core):
        i = lax.rem(r + 4 * d + 16, 16)
        i = i if own_h else i + 2 - 4 * x_hi
        return i if own_core else i + 1 - 2 * core

    reach_z = {True: (4, 3), False: (3, 4)}
    reach_y = {True: (2, 1), False: (1, 2)}

    def zsend(d, own, sign):
        if abs(d) < reach_z[own][0 if sign > 0 else 1]:
            here = rows.at[0, rslot(d, own)]
            start(here, here, to_zp if sign > 0 else to_zm, ("z", sign, abs(d) + 1, own))

    def ysend(t, d, own_h, sign):
        if abs(d) < reach_y[own_h][0 if sign > 0 else 1]:
            here = cols.at[t, cslot(d, own_h, True)]
            start(here, here, to_yp if sign > 0 else to_ym, ("y", t, sign, abs(d) + 1, own_h))

    I_EVENTS = [(0, True), (0, False)]
    for s in (1, 2, 3):
        I_EVENTS += [(-s, True), (s, True), (-s, False), (s, False)]
    I_EVENTS += [(-4, True), (4, False)]
    C_EVENTS = [(0, True), (0, False), (-1, True), (1, True), (-1, False), (1, False), (-2, True), (2, False)]

    def i_event(e):
        d, own = I_EVENTS[e]
        here = rows.at[0, rslot(d, own)]
        if e == 0:
            start(here, here, to_x, ("x",))
        elif e == 1:
            arrived(here, ("x",))
        else:
            arrived(here, ("z", 1 if d < 0 else -1, abs(d), own))
        if d <= 0:
            zsend(d, own, 1)
        if d >= 0:
            zsend(d, own, -1)

    def c_event(t, n):
        d, own_h = C_EVENTS[n]
        here = cols.at[t, cslot(d, own_h, True)]
        if n == 0:
            start(here, here, to_h, ("h", t))
        elif n == 1:
            arrived(here, ("h", t))
        else:
            arrived(here, ("y", t, 1 if d < 0 else -1, abs(d), own_h))
        if d <= 0:
            ysend(t, d, own_h, 1)
        if d >= 0:
            ysend(t, d, own_h, -1)
        start(here, here, to_core, ("core", t, n))

    def core_event(t, n):
        d, own_h = C_EVENTS[n]
        arrived(cols.at[t, cslot(d, own_h, False)], ("core", t, n))

    FAR_SEND, FAR_RECV = ids(send_ids, ("a", 4)), ids(recv_ids, ("a", 4))

    def far_copy(sign):
        here = rows.at[1, rslot(-3 * sign, True)]
        return copy(here, here, to_zp if sign > 0 else to_zm, FAR_SEND, FAR_RECV)

    def a_event(d):
        here = rows.at[1, rslot(d, True)]
        if d == 4:
            wait_at(here, FAR_RECV)
        elif d:
            arrived(here, ("a", 1 if d < 0 else -1, abs(d)))
        for sign in (1, -1):
            if d * sign <= 0:
                if abs(d) < 3:
                    start(here, here, to_zp if sign > 0 else to_zm, ("a", sign, abs(d) + 1))
                elif abs(d) == 3:
                    @pl.when(core == (0 if sign > 0 else 1))
                    def _():
                        far_copy(sign).start()
        start(here, here, to_x, ("ax", d))

    def ax_event(d):
        arrived(rows.at[1, rslot(d, False)], ("ax", d))

    Y_RECV, Y_SEND = ids(recv_ids, ("ty",), 8), ids(send_ids, ("ty",), 8)
    Z_RECV, Z_SEND = ids(recv_ids, ("tz",), 16), ids(send_ids, ("tz",), 8)
    F_RECV, F_SEND = ids(recv_ids, ("tf",), 8), ids(send_ids, ("tf",), 16)

    def cut(k):
        return pl.ds(pl.multiple_of(k * PIECE, PIECE), PIECE)

    def own_tile(t):
        return cols.at[0, r] if t == 0 else rows.at[0, c]

    def y_copy(t, dk):
        k = lax.rem(y + dk, 4)
        return copy(own_tile(t).at[:, cut(k)], stage_y.at[t, y], (lax.rem(r + 4 * dk, 16), c),
                    Y_SEND + 4 * t + dk, Y_RECV + 4 * t + dk)

    def z_copy(t, dk):
        from_y = lax.rem(y - dk + 4, 4)
        to = 2 * from_y + x_hi
        return to, copy(stage_y.at[t, from_y], stage_z.at[t, z], (r, 2 * to + x_lo), Z_SEND + 4 * t + dk, Z_RECV + 8 * t + z)

    def y_start(t):
        for dk in (1, 3, 2):
            y_copy(t, dk).start()
        stage_y[t, y] = own_tile(t)[:, cut(y)]
        z_start(t, 0)

    def z_start(t, dk):
        from_y = lax.rem(y - dk + 4, 4)
        if dk:
            wait_at(stage_y.at[t, from_y], Y_RECV + 4 * t + dk)
        to, op = z_copy(t, dk)

        @pl.when(to != z)
        def _():
            op.start()

        @pl.when(to == z)
        def _():
            stage_z[t, z] = stage_y[t, from_y]

    def f_copy(t, d):
        from_z = lax.rem(z + d + 8, 8)
        where = (2 * from_z + x_lo, 2 * z + core)
        src = stage_z.at[t, from_z]
        if t == 0:
            dst = rows.at[1, 2 * z + core, :, cut(y)]
        else:
            dst = cols.at[1, 2 * from_z + x_lo, :, cut(y)]
        stays = (where[0] == r) & (where[1] == c)
        return stays, dst, copy(src, dst, where, F_SEND + 8 * t + (d + 8) % 8, F_RECV + 4 * t + y)

    def f_start(t, ds):
        @pl.when(relay)
        def _():
            for d in ds:
                from_z = lax.rem(z + d + 8, 8)
                if d:
                    wait_at(stage_z.at[t, from_z], Z_RECV + 8 * t + from_z)
                stays, dst, op = f_copy(t, d)

                @pl.when(jnp.logical_not(stays))
                def _():
                    op.start()

                @pl.when(stays)
                def _():
                    dst[...] = stage_z[t, from_z]

    def f_arrived(t):
        for k in range(4):
            dst = rows.at[1, c, :, cut(k)] if t == 0 else cols.at[1, r, :, cut(k)]

            @pl.when(jnp.logical_not(at_home & (y == k)))
            def _():
                wait_at(dst, F_RECV + 4 * t + k)

    def exchange_sent():
        for t in (0, 1):
            for dk in (1, 2, 3):
                y_copy(t, dk).wait_send()
            for dk in range(4):
                to, op = z_copy(t, dk)

                @pl.when(to != z)
                def _():
                    op.wait_send()

            @pl.when(relay)
            def _():
                for d in range(8):
                    stays, _, op = f_copy(t, d)

                    @pl.when(jnp.logical_not(stays))
                    def _():
                        op.wait_send()

    tile = 256
    target = (out_ref, acc)

    def term(t, ds, m):
        span = pl.ds(pl.multiple_of(m * tile, tile), tile)
        blocks = [2 * lax.rem(z + d + 8, 8) for d in ds]
        left = jnp.concatenate([rows[t, pl.ds(b, 2), :, span].reshape(192, tile) for b in blocks], 0)
        right = jnp.concatenate([cols[t, pl.ds(b, 2)].reshape(192, 1536) for b in blocks], 0)
        return lax.dot_general(left, right, (((0,), (0,)), ((), ())), preferred_element_type=jnp.float32)

    def product(t, ds, lo, hi, first):
        dest = target[t]

        @pl.loop(lo, hi)
        def _(m):
            span = pl.ds(pl.multiple_of(m * tile, tile), tile)
            if first:
                dest[span, :] = term(t, ds, m)
            else:
                dest[span, :] = dest[span, :] + term(t, ds, m)

    NEAR, FAR = (0, -1, 1, -2), (2, -3, 3, 4)

    load_i = pltpu.make_async_copy(i_ref, rows.at[0, c], load_sems.at[0])
    load_a = pltpu.make_async_copy(a_ref, cols.at[0, r], load_sems.at[1])
    load_i.start()
    load_a.start()
    barrier = pltpu.get_barrier_semaphore()

    def greet(device):
        pl.semaphore_signal(barrier, inc=1, device_id=device, device_id_type=MESH)

    for device in (to_x, to_zp, to_zm, to_h, to_yp, to_ym, to_y2, to_core):
        greet(device)

    @pl.when(relay)
    def _():
        for d in range(1, 8):
            greet((r, 2 * lax.rem(z + d, 8) + x_lo))

    for k in range(4):
        @pl.when(jnp.logical_not(at_home & (y == k)))
        def _():
            greet((4 * k + 2 * lax.rem(z, 2) + x_lo, 2 * z + core))

    load_i.wait()
    load_a.wait()

    @pl.when(jnp.logical_not(relay))
    def _():
        pl.semaphore_wait(barrier, 12)

    @pl.when(relay & jnp.logical_not(at_home))
    def _():
        pl.semaphore_wait(barrier, 19)

    @pl.when(at_home)
    def _():
        pl.semaphore_wait(barrier, 18)

    events = [
        (0, lambda: y_start(0)), (0.1, lambda: i_event(0)), (0.2, lambda: c_event(0, 0)), (0.3, lambda: y_start(1)),
        (4, lambda: i_event(1)), (4.5, lambda: z_start(0, 1)), (4.6, lambda: z_start(0, 3)), (5, lambda: z_start(0, 2)),
        (6, lambda: c_event(0, 1)), (8, lambda: z_start(1, 1)), (8.1, lambda: z_start(1, 3)), (8.2, lambda: z_start(1, 2)),
        (11, lambda: c_event(0, 2)), (11.1, lambda: c_event(0, 3)),
        (12, lambda: i_event(2)), (12.1, lambda: i_event(3)),
        (13, lambda: f_start(0, (0, -1, 1, -2, 2))), (15, lambda: f_start(0, (-3, 3, 4))),
        (18, lambda: i_event(4)), (18.1, lambda: i_event(5)), (18.2, lambda: c_event(0, 4)), (18.3, lambda: c_event(0, 5)),
        (20, lambda: f_start(1, (0, -1, 1, -2, 2))), (21, lambda: f_start(1, (-3, 3, 4))),
        (24, lambda: i_event(6)), (24.1, lambda: i_event(7)),
        (25, lambda: c_event(0, 6)), (25.1, lambda: c_event(0, 7)),
        (26, lambda: f_arrived(0)), (26.1, lambda: a_event(0)),
        (29, lambda: f_arrived(1)), (29.1, lambda: c_event(1, 0)),
        (30, lambda: i_event(8)), (30.1, lambda: i_event(9)),
        (36, lambda: c_event(1, 1)), (36.1, lambda: a_event(-1)), (36.2, lambda: a_event(1)),
        (40, lambda: i_event(10)), (40.1, lambda: i_event(11)),
        (42, lambda: c_event(1, 2)), (42.1, lambda: c_event(1, 3)),
        (48, lambda: a_event(-2)), (48.1, lambda: a_event(2)), (49, lambda: c_event(1, 4)), (49.1, lambda: c_event(1, 5)),
        (52, lambda: i_event(12)), (52.1, lambda: i_event(13)),
        (56, lambda: c_event(1, 6)), (56.1, lambda: c_event(1, 7)),
        (60, lambda: a_event(-3)), (60.1, lambda: a_event(3)),
        (64, lambda: i_event(14)), (64.1, lambda: i_event(15)),
        (70, lambda: a_event(4)),
    ]
    for n in range(8):
        events.append((31, lambda n=n: core_event(0, n)))
        events.append((66, lambda n=n: core_event(1, n)))
    for m, at in enumerate((37, 41, 43, 50, 53, 57)):
        events.append((at, lambda m=m: product(0, NEAR, m, m + 1, True)))
    events.append((65, lambda: product(0, FAR, 0, 6, False)))
    for d in (0, -1, 1, -2):
        events.append((66.5, lambda d=d: ax_event(d)))
    events.append((67, lambda: product(1, NEAR, 0, 6, True)))
    for d in (2, -3, 3, 4):
        events.append((71, lambda d=d: ax_event(d)))
    for _, event in sorted(events, key=lambda item: item[0]):
        event()

    @pl.loop(0, 1536 // tile)
    def _(m):
        span = pl.ds(pl.multiple_of(m * tile, tile), tile)
        half = (acc[span, :] + term(1, FAR, m)).astype(jnp.bfloat16)
        out_ref[span, :] = out_ref[span, :] + half.astype(jnp.float32)

    for op in plain:
        op.wait_send()
    far_copy(1).wait_send()
    exchange_sent()


def scale_kernel(sum_ref, row_e_ref, col_e_ref, out_ref, buffer, sems):
    tile = buffer.shape[1]
    steps = sum_ref.shape[0] // tile

    def put(m, slot):
        return pltpu.make_async_copy(
            buffer.at[slot], out_ref.at[pl.ds(pl.multiple_of(m * tile, tile), tile), :], sems.at[slot])

    @pl.loop(0, steps)
    def _(m):
        slot = lax.rem(m, 2)

        @pl.when(m >= 2)
        def _():
            put(m - 2, slot).wait()

        span = pl.ds(pl.multiple_of(m * tile, tile), tile)
        buffer[slot] = sum_ref[span, :] / (row_e_ref[span, :] + col_e_ref[...])
        put(m, slot).start()

    put(steps - 2, (steps - 2) % 2).wait()
    put(steps - 1, (steps - 1) % 2).wait()


def body(integrals, amplitudes, energies):
    size = integrals.shape[0]
    depth = amplitudes.shape[0]
    n = lax.axis_size("col")
    summed = pl.pallas_call(
        gather_kernel,
        out_shape=jax.ShapeDtypeStruct((size, size), jnp.float32),
        in_specs=[pl.BlockSpec(memory_space=pl.ANY)] * 2,
        out_specs=pl.BlockSpec(memory_space=pltpu.VMEM),
        scratch_shapes=[
            pltpu.VMEM((2, n, depth, size), jnp.bfloat16),
            pltpu.VMEM((2, n, depth, size), jnp.bfloat16),
            pltpu.VMEM((size, size), jnp.float32),
            pltpu.VMEM((2, 4, depth, PIECE), jnp.bfloat16),
            pltpu.VMEM((2, 8, depth, PIECE), jnp.bfloat16),
            pltpu.SemaphoreType.DMA((2,)),
            pltpu.SemaphoreType.DMA((N_SEND,)),
            pltpu.SemaphoreType.DMA((N_RECV,)),
        ],
        compiler_params=pltpu.CompilerParams(
            collective_id=0, has_side_effects=True, vmem_limit_bytes=44 * MIB),
    )(integrals.T, amplitudes)
    row_e = lax.dynamic_slice_in_dim(energies, lax.axis_index("row") * size, size, 0)[:, None]
    col_e = lax.dynamic_slice_in_dim(energies, lax.axis_index("col") * size, size, 0)[None, :]
    return pl.pallas_call(
        scale_kernel,
        out_shape=jax.ShapeDtypeStruct((size, size), jnp.float32),
        in_specs=[pl.BlockSpec(memory_space=pltpu.VMEM)] * 3,
        out_specs=pl.BlockSpec(memory_space=pl.ANY),
        scratch_shapes=[
            pltpu.VMEM((2, 128, size), jnp.float32),
            pltpu.SemaphoreType.DMA((2,)),
        ],
        compiler_params=pltpu.CompilerParams(vmem_limit_bytes=16 * MIB),
    )(summed, row_e, col_e)


def solution(mesh):
    return jax.shard_map(
        body,
        mesh=mesh,
        in_specs=(P("row", "col"), P("row", "col"), P()),
        out_specs=P("row", "col"),
        check_vma=False,
    )
```

```python
import functools

import jax
import jax.numpy as jnp
from jax import lax
from jax.experimental import pallas as pl
from jax.experimental.pallas import tpu as pltpu
from jax.sharding import PartitionSpec as P

MESH = pl.DeviceIdType.MESH
N_SEND = 192
N_RECV = 128
MIB = 1 << 20
PIECE = 384


def gather_kernel(i_ref, a_ref, ladder, partner, rows1, cols1, rows0, cols0, stage_p, stage_z, load_sems, send_sems, recv_sems):
    rows, cols = (rows0, rows1), (cols0, cols1)
    r, c = lax.axis_index("row"), lax.axis_index("col")
    x_lo, x_hi, core = lax.rem(c, 2), lax.rem(r // 2, 2), lax.rem(r, 2)
    z, y = c // 2, r // 4
    to_x = (r, c + 1 - 2 * x_lo)
    to_zp, to_zm = (r, lax.rem(c + 2, 16)), (r, lax.rem(c + 14, 16))
    to_h = (r + 2 - 4 * x_hi, c)
    to_yp, to_ym = (lax.rem(r + 4, 16), c), (lax.rem(r + 12, 16), c)
    to_y2 = (lax.rem(r + 8, 16), c)
    to_core = (r + 1 - 2 * core, c)
    relay = x_hi == lax.rem(z, 2)
    at_home = relay & (core == x_lo)

    send_ids, recv_ids, plain = {}, {}, []

    def ids(table, key, count=1):
        if key not in table:
            table[key] = sum(n for _, n in table.values()), count
        return table[key][0]

    def copy(src, dst, device, send, recv):
        return pltpu.make_async_remote_copy(
            src_ref=src, dst_ref=dst, send_sem=send_sems.at[send], recv_sem=recv_sems.at[recv],
            device_id=device, device_id_type=MESH)

    def start(src, dst, device, key):
        op = copy(src, dst, device, ids(send_ids, key), ids(recv_ids, key))
        op.start()
        plain.append(op)

    def wait_at(dst, recv):
        copy(dst, dst, to_x, 0, recv).wait_recv()

    def arrived(dst, key):
        wait_at(dst, ids(recv_ids, key))

    def rslot(d, own):
        j = lax.rem(c + 2 * d + 16, 16)
        return j if own else j + 1 - 2 * lax.rem(j, 2)

    def cslot(d, own_h, own_core):
        i = lax.rem(r + 4 * d + 16, 16)
        i = i if own_h else i + 2 - 4 * x_hi
        return i if own_core else i + 1 - 2 * core

    reach_z = {True: (4, 3), False: (3, 4)}
    reach_y = {True: (2, 1), False: (1, 2)}

    def zsend(d, own, sign):
        if abs(d) < reach_z[own][0 if sign > 0 else 1]:
            here = rows[1].at[rslot(d, own)]
            start(here, here, to_zp if sign > 0 else to_zm, ("z", sign, abs(d) + 1, own))

    def ysend(t, d, own_h, sign):
        if abs(d) < reach_y[own_h][0 if sign > 0 else 1]:
            here = cols[t].at[cslot(d, own_h, True)]
            start(here, here, to_yp if sign > 0 else to_ym, ("y", t, sign, abs(d) + 1, own_h))

    A_EVENTS = [(0, True), (0, False)]
    for s in (1, 2, 3):
        A_EVENTS += [(-s, True), (s, True), (-s, False), (s, False)]
    A_EVENTS += [(-4, True), (4, False)]
    C_EVENTS = [(0, True), (0, False), (-1, True), (1, True), (-1, False), (1, False), (-2, True), (2, False)]

    def a_event(e):
        d, own = A_EVENTS[e]
        here = rows[1].at[rslot(d, own)]
        if e == 0:
            start(here, here, to_x, ("x",))
        elif e == 1:
            arrived(here, ("x",))
        else:
            arrived(here, ("z", 1 if d < 0 else -1, abs(d), own))
        if d <= 0:
            zsend(d, own, 1)
        if d >= 0:
            zsend(d, own, -1)

    def c_event(t, n):
        d, own_h = C_EVENTS[n]
        here = cols[t].at[cslot(d, own_h, True)]
        if n == 0:
            start(here, here, to_h, ("h", t))
        elif n == 1:
            arrived(here, ("h", t))
        else:
            arrived(here, ("y", t, 1 if d < 0 else -1, abs(d), own_h))
        if d <= 0:
            ysend(t, d, own_h, 1)
        if d >= 0:
            ysend(t, d, own_h, -1)
        start(here, here, to_core, ("core", t, n))

    def core_event(t, n):
        d, own_h = C_EVENTS[n]
        arrived(cols[t].at[cslot(d, own_h, False)], ("core", t, n))

    FAR_SEND, FAR_RECV = ids(send_ids, ("i", 4)), ids(recv_ids, ("i", 4))

    def far_copy(sign):
        here = rows[0].at[rslot(-3 * sign, True)]
        return copy(here, here, to_zp if sign > 0 else to_zm, FAR_SEND, FAR_RECV)

    def i_event(d):
        here = rows[0].at[rslot(d, True)]
        if d == 4:
            wait_at(here, FAR_RECV)
        elif d:
            arrived(here, ("i", 1 if d < 0 else -1, abs(d)))
        for sign in (1, -1):
            if d * sign <= 0:
                if abs(d) < 3:
                    start(here, here, to_zp if sign > 0 else to_zm, ("i", sign, abs(d) + 1))
                elif abs(d) == 3:
                    @pl.when(core == (0 if sign > 0 else 1))
                    def _():
                        far_copy(sign).start()

    def ix_start(d):
        here = rows[0].at[rslot(d, True)]
        start(here, here, to_x, ("ix", d))

    def ix_event(d):
        arrived(rows[0].at[rslot(d, False)], ("ix", d))

    P_RECV, P_SEND = ids(recv_ids, ("tp",), 16), ids(send_ids, ("tp",), 8)
    Z_RECV, Z_SEND = ids(recv_ids, ("tz",), 8), ids(send_ids, ("tz",), 16)
    F_RECV, F_SEND = ids(recv_ids, ("tf",), 8), ids(send_ids, ("tf",), 8)

    def cut(k):
        return pl.ds(pl.multiple_of(k * PIECE, PIECE), PIECE)

    def own_tile(t):
        return cols[0].at[r] if t == 0 else rows[0].at[c]

    def p_copy(t, dk):
        k = lax.rem(y + dk, 4)
        return copy(own_tile(t).at[:, cut(k)], stage_p.at[t, r // 2], (4 * k + 2 * lax.rem(z, 2) + x_lo, 2 * z + core),
                    P_SEND + 4 * t + dk, P_RECV + 8 * t + r // 2)

    def p_start(t):
        for dk in (1, 3, 2):
            p_copy(t, dk).start()

        @pl.when(at_home)
        def _():
            stage_p[t, r // 2] = own_tile(t)[:, cut(y)]

        @pl.when(jnp.logical_not(at_home))
        def _():
            p_copy(t, 0).start()

    def z_copy(t, d):
        to = lax.rem(z + d + 8, 8)
        return to, copy(stage_p.at[t, to], stage_z.at[t, z // 2], (r, 2 * to + x_lo), Z_SEND + 8 * t + (d + 8) % 8, Z_RECV + 4 * t + z // 2)

    def z_start(t, ds):
        @pl.when(relay)
        def _():
            for d in ds:
                to, op = z_copy(t, d)

                @pl.when(jnp.logical_not(at_home & (to == r // 2)))
                def _():
                    wait_at(stage_p.at[t, to], P_RECV + 8 * t + to)

                if d:
                    op.start()
                else:
                    stage_z[t, z // 2] = stage_p[t, z]

    def f_copy(t, dz):
        part = lax.rem(y + dz, 4)
        dst = rows[1].at[c, :, cut(y)] if t == 0 else cols[1].at[4 * part + 2 * x_hi + core, :, cut(y)]
        return part, dst, copy(stage_z.at[t, part], dst, (4 * part + 2 * x_hi + core, c), F_SEND + 4 * t + dz, F_RECV + 4 * t + y)

    def f_start(t):
        for dz in (0, 1, 3, 2):
            part, dst, op = f_copy(t, dz)

            @pl.when(jnp.logical_not(relay & (part == z // 2)))
            def _():
                wait_at(stage_z.at[t, part], Z_RECV + 4 * t + part)

            if dz:
                op.start()
            else:
                dst[...] = stage_z[t, part]

    def f_arrived(t):
        for dk in (1, 3, 2):
            k = lax.rem(y + dk, 4)
            wait_at(rows[1].at[c, :, cut(k)] if t == 0 else cols[1].at[r, :, cut(k)], F_RECV + 4 * t + k)

    def exchange_sent():
        for t in (0, 1):
            for dk in (1, 2, 3):
                p_copy(t, dk).wait_send()
                f_copy(t, dk)[2].wait_send()

            @pl.when(jnp.logical_not(at_home))
            def _():
                p_copy(t, 0).wait_send()

            @pl.when(relay)
            def _():
                for d in range(1, 8):
                    z_copy(t, d)[1].wait_send()

    tile = 256
    target = (ladder, partner)

    def term(t, ds, m):
        span = pl.ds(pl.multiple_of(m * tile, tile), tile)
        blocks = [2 * lax.rem(z + d + 8, 8) for d in ds]
        left = jnp.concatenate([rows[t][pl.ds(b, 2), :, span].reshape(192, tile) for b in blocks], 0)
        right = jnp.concatenate([cols[t][pl.ds(b, 2)].reshape(192, 1536) for b in blocks], 0)
        return lax.dot_general(left, right, (((0,), (0,)), ((), ())), preferred_element_type=jnp.float32)

    def product(t, ds, lo, hi, first):
        dest = target[t]

        @pl.loop(lo, hi)
        def _(m):
            span = pl.ds(pl.multiple_of(m * tile, tile), tile)
            if first:
                dest[span, :] = term(t, ds, m)
            else:
                dest[span, :] = dest[span, :] + term(t, ds, m)

    NEAR, MID, LAST = (0, -1, 1, -2), (2, -3, 3), (4,)

    load_i = pltpu.make_async_copy(i_ref, rows0.at[c], load_sems.at[0])
    load_a = pltpu.make_async_copy(a_ref, cols0.at[r], load_sems.at[1])
    load_i.start()
    load_a.start()
    barrier = pltpu.get_barrier_semaphore()

    def greet(device):
        pl.semaphore_signal(barrier, inc=1, device_id=device, device_id_type=MESH)

    for device in (to_x, to_zp, to_zm, to_h, to_yp, to_ym, to_y2, to_core):
        greet(device)

    @pl.when(relay)
    def _():
        for k in range(8):
            @pl.when(jnp.logical_not(at_home & (r // 2 == k)))
            def _():
                greet((2 * k + x_lo, 2 * z + core))

    for k in range(4):
        @pl.when(z != 2 * k + x_hi)
        def _():
            greet((r, 4 * k + 2 * x_hi + x_lo))

    load_i.wait()
    load_a.wait()

    @pl.when(jnp.logical_not(relay))
    def _():
        pl.semaphore_wait(barrier, 12)

    @pl.when(relay & jnp.logical_not(at_home))
    def _():
        pl.semaphore_wait(barrier, 19)

    @pl.when(at_home)
    def _():
        pl.semaphore_wait(barrier, 18)

    ORDER = (0, -1, 1, -2, 2, -3, 3, 4)
    events = [
        (0, lambda: p_start(0)), (0.1, lambda: i_event(0)), (0.2, lambda: p_start(1)), (0.3, lambda: ix_start(0)),
        (0.4, lambda: c_event(0, 0)),
        (9, lambda: z_start(0, ORDER)),
        (11, lambda: i_event(-1)), (11.1, lambda: i_event(1)), (11.2, lambda: ix_start(-1)), (11.3, lambda: ix_start(1)),
        (14, lambda: z_start(1, ORDER)),
        (16, lambda: f_start(0)),
        (18, lambda: c_event(0, 1)), (18.1, lambda: c_event(0, 2)), (18.2, lambda: c_event(0, 3)),
        (19, lambda: i_event(-2)), (19.1, lambda: i_event(2)), (19.2, lambda: ix_start(-2)), (19.3, lambda: ix_start(2)),
        (21, lambda: f_arrived(0)), (21.1, lambda: a_event(0)),
        (23, lambda: f_start(1)),
        (26, lambda: c_event(0, 4)), (26.1, lambda: c_event(0, 5)),
        (27, lambda: i_event(-3)), (27.1, lambda: i_event(3)),
        (28, lambda: a_event(1)), (28.1, lambda: ix_start(-3)), (28.2, lambda: ix_start(3)),
        (29, lambda: f_arrived(1)), (29.1, lambda: c_event(1, 0)),
        (33, lambda: i_event(4)), (33.1, lambda: ix_start(4)), (34, lambda: c_event(0, 6)), (34.1, lambda: c_event(0, 7)),
        (36, lambda: a_event(2)), (36.1, lambda: a_event(3)), (38, lambda: c_event(1, 1)),
        (42, lambda: a_event(4)), (42.1, lambda: a_event(5)), (43, lambda: c_event(1, 2)), (43.1, lambda: c_event(1, 3)),
        (49, lambda: a_event(6)), (49.1, lambda: a_event(7)), (51, lambda: c_event(1, 4)), (51.1, lambda: c_event(1, 5)),
        (55, lambda: a_event(8)), (55.1, lambda: a_event(9)), (58, lambda: c_event(1, 6)), (58.1, lambda: c_event(1, 7)),
        (61, lambda: a_event(10)), (61.1, lambda: a_event(11)),
        (68, lambda: a_event(12)), (68.1, lambda: a_event(13)),
        (75, lambda: a_event(14)), (76, lambda: a_event(15)),
    ]
    for n in range(8):
        events.append((40, lambda n=n: core_event(0, n)))
        events.append((64, lambda n=n: core_event(1, n)))
    for d in NEAR:
        events.append((44, lambda d=d: ix_event(d)))
    for d in MID + LAST:
        events.append((57, lambda d=d: ix_event(d)))
    for m in range(6):
        events.append(((45, 46, 47, 50, 52, 53)[m], lambda m=m: product(0, NEAR, m, m + 1, True)))
        events.append(((57.5, 59, 60, 62, 63, 64)[m], lambda m=m: product(0, MID + LAST, m, m + 1, False)))
    events.append((65, lambda: product(1, NEAR, 0, 3, True)))
    events.append((69, lambda: product(1, NEAR, 3, 6, True)))
    events.append((70, lambda: product(1, MID, 0, 6, False)))
    for _, event in sorted(events, key=lambda item: item[0]):
        event()
    for op in plain:
        op.wait_send()
    far_copy(1).wait_send()
    exchange_sent()


def finish_kernel(ladder, partner, rows1, cols1, energies, out_ref, buffer, sems):
    r, c = lax.axis_index("row"), lax.axis_index("col")
    last = 2 * lax.rem(c // 2 + 4, 8)
    tile, slots, wide = buffer.shape[1], buffer.shape[0], 512
    size = ladder.shape[0]
    steps = size // tile
    per = size // 128

    def put(m, slot):
        return pltpu.make_async_copy(
            buffer.at[slot], out_ref.at[pl.ds(pl.multiple_of(m * tile, tile), tile), :], sems.at[slot])

    @pl.loop(0, steps)
    def _(m):
        slot = lax.rem(m, slots)

        @pl.when(m >= slots)
        def _():
            put(m - slots, slot).wait()

        span = pl.ds(pl.multiple_of(m * tile, tile), tile)
        left = rows1[pl.ds(last, 2), :, span].reshape(192, tile)
        row_e = jnp.broadcast_to(energies[pl.ds(r * per + m, 1), :], (128, 128)).T
        for n in range(size // wide):
            there = slice(n * wide, (n + 1) * wide)
            right = cols1[pl.ds(last, 2), :, there].reshape(192, wide)
            term = lax.dot_general(left, right, (((0,), (0,)), ((), ())), preferred_element_type=jnp.float32)
            half = (partner[span, there] + term).astype(jnp.bfloat16).astype(jnp.float32)
            total = ladder[span, there] + half
            for j in range(wide // 128):
                denom = row_e + energies[pl.ds(c * per + n * (wide // 128) + j, 1), :]
                inverse = pl.reciprocal(denom, approx=True)
                inverse = inverse * (2.0 - denom * inverse)
                at = n * wide + j * 128
                buffer[slot, :, at:at + 128] = total[:, j * 128:(j + 1) * 128] * inverse
        put(m, slot).start()

    for m in range(steps - slots, steps):
        put(m, m % slots).wait()


def body(integrals, amplitudes, energies):
    size = integrals.shape[0]
    depth = amplitudes.shape[0]
    n = lax.axis_size("col")
    panel = jax.ShapeDtypeStruct((n, depth, size), jnp.bfloat16)
    block = jax.ShapeDtypeStruct((size, size), jnp.float32)
    ladder, partner, rows1, cols1 = pl.pallas_call(
        gather_kernel,
        out_shape=(block, block, panel, panel),
        in_specs=[pl.BlockSpec(memory_space=pltpu.HBM)] * 2,
        out_specs=(pl.BlockSpec(memory_space=pltpu.VMEM),) * 4,
        scratch_shapes=[
            pltpu.VMEM((n, depth, size), jnp.bfloat16),
            pltpu.VMEM((n, depth, size), jnp.bfloat16),
            pltpu.VMEM((2, 8, depth, PIECE), jnp.bfloat16),
            pltpu.VMEM((2, 4, depth, PIECE), jnp.bfloat16),
            pltpu.SemaphoreType.DMA((2,)),
            pltpu.SemaphoreType.DMA((N_SEND,)),
            pltpu.SemaphoreType.DMA((N_RECV,)),
        ],
        compiler_params=pltpu.CompilerParams(
            collective_id=0, has_side_effects=True, vmem_limit_bytes=25_000_000),
    )(integrals.T, amplitudes)
    return pl.pallas_call(
        finish_kernel,
        out_shape=block,
        in_specs=[pl.BlockSpec(memory_space=pltpu.VMEM)] * 5,
        out_specs=pl.BlockSpec(memory_space=pl.ANY),
        scratch_shapes=[
            pltpu.VMEM((3, 128, size), jnp.float32),
            pltpu.SemaphoreType.DMA((3,)),
        ],
        compiler_params=pltpu.CompilerParams(vmem_limit_bytes=16 * MIB),
    )(ladder, partner, rows1, cols1, energies.reshape(-1, 128))


def solution(mesh):
    return jax.shard_map(
        body,
        mesh=mesh,
        in_specs=(P("row", "col"), P("row", "col"), P()),
        out_specs=P("row", "col"),
        check_vma=False,
    )
```

```python
import functools

import jax
import jax.numpy as jnp
from jax import lax
from jax.experimental import pallas as pl
from jax.experimental.pallas import tpu as pltpu
from jax.sharding import PartitionSpec as P

MESH = pl.DeviceIdType.MESH
N_SEND = 192
N_RECV = 128
MIB = 1 << 20
PIECE = 384


def gather_kernel(i_ref, a_ref, ladder, partner, rows1, cols1, rows0, cols0, stage_p, stage_z, load_sems, send_sems, recv_sems):
    rows, cols = (rows0, rows1), (cols0, cols1)
    r, c = lax.axis_index("row"), lax.axis_index("col")
    x_lo, x_hi, core = lax.rem(c, 2), lax.rem(r // 2, 2), lax.rem(r, 2)
    z, y = c // 2, r // 4
    to_x = (r, c + 1 - 2 * x_lo)
    to_zp, to_zm = (r, lax.rem(c + 2, 16)), (r, lax.rem(c + 14, 16))
    to_h = (r + 2 - 4 * x_hi, c)
    to_yp, to_ym = (lax.rem(r + 4, 16), c), (lax.rem(r + 12, 16), c)
    to_y2 = (lax.rem(r + 8, 16), c)
    to_core = (r + 1 - 2 * core, c)
    relay = x_hi == lax.rem(z, 2)
    at_home = relay & (core == x_lo)

    send_ids, recv_ids, plain = {}, {}, []

    def ids(table, key, count=1):
        if key not in table:
            table[key] = sum(n for _, n in table.values()), count
        return table[key][0]

    def copy(src, dst, device, send, recv):
        return pltpu.make_async_remote_copy(
            src_ref=src, dst_ref=dst, send_sem=send_sems.at[send], recv_sem=recv_sems.at[recv],
            device_id=device, device_id_type=MESH)

    def start(src, dst, device, key):
        op = copy(src, dst, device, ids(send_ids, key), ids(recv_ids, key))
        op.start()
        plain.append(op)

    def wait_at(dst, recv):
        copy(dst, dst, to_x, 0, recv).wait_recv()

    def arrived(dst, key):
        wait_at(dst, ids(recv_ids, key))

    def rslot(d, own):
        j = lax.rem(c + 2 * d + 16, 16)
        return j if own else j + 1 - 2 * lax.rem(j, 2)

    def cslot(d, own_h, own_core):
        i = lax.rem(r + 4 * d + 16, 16)
        i = i if own_h else i + 2 - 4 * x_hi
        return i if own_core else i + 1 - 2 * core

    reach_z = {True: (4, 3), False: (3, 4)}
    reach_y = {True: (2, 1), False: (1, 2)}

    def zsend(d, own, sign):
        if abs(d) < reach_z[own][0 if sign > 0 else 1]:
            here = rows[1].at[rslot(d, own)]
            start(here, here, to_zp if sign > 0 else to_zm, ("z", sign, abs(d) + 1, own))

    def ysend(t, d, own_h, sign):
        if abs(d) < reach_y[own_h][0 if sign > 0 else 1]:
            here = cols[t].at[cslot(d, own_h, True)]
            start(here, here, to_yp if sign > 0 else to_ym, ("y", t, sign, abs(d) + 1, own_h))

    A_EVENTS = [(0, True), (0, False)]
    for s in (1, 2, 3):
        A_EVENTS += [(-s, True), (s, True), (-s, False), (s, False)]
    A_EVENTS += [(-4, True), (4, False)]
    C_EVENTS = [(0, True), (0, False), (-1, True), (1, True), (-1, False), (1, False), (-2, True), (2, False)]

    def a_event(e):
        d, own = A_EVENTS[e]
        here = rows[1].at[rslot(d, own)]
        if e == 0:
            start(here, here, to_x, ("x",))
        elif e == 1:
            arrived(here, ("x",))
        else:
            arrived(here, ("z", 1 if d < 0 else -1, abs(d), own))
        if d <= 0:
            zsend(d, own, 1)
        if d >= 0:
            zsend(d, own, -1)

    def c_event(t, n):
        d, own_h = C_EVENTS[n]
        here = cols[t].at[cslot(d, own_h, True)]
        if n == 0:
            start(here, here, to_h, ("h", t))
        elif n == 1:
            arrived(here, ("h", t))
        else:
            arrived(here, ("y", t, 1 if d < 0 else -1, abs(d), own_h))
        if d <= 0:
            ysend(t, d, own_h, 1)
        if d >= 0:
            ysend(t, d, own_h, -1)
        start(here, here, to_core, ("core", t, n))

    def core_event(t, n):
        d, own_h = C_EVENTS[n]
        arrived(cols[t].at[cslot(d, own_h, False)], ("core", t, n))

    FAR_SEND, FAR_RECV = ids(send_ids, ("i", 4)), ids(recv_ids, ("i", 4))

    def far_copy(sign):
        here = rows[0].at[rslot(-3 * sign, True)]
        return copy(here, here, to_zp if sign > 0 else to_zm, FAR_SEND, FAR_RECV)

    def i_event(d):
        here = rows[0].at[rslot(d, True)]
        if d == 4:
            wait_at(here, FAR_RECV)
        elif d:
            arrived(here, ("i", 1 if d < 0 else -1, abs(d)))
        for sign in (1, -1):
            if d * sign <= 0:
                if abs(d) < 3:
                    start(here, here, to_zp if sign > 0 else to_zm, ("i", sign, abs(d) + 1))
                elif abs(d) == 3:
                    @pl.when(core == (0 if sign > 0 else 1))
                    def _():
                        far_copy(sign).start()

    def ix_start(d):
        here = rows[0].at[rslot(d, True)]
        start(here, here, to_x, ("ix", d))

    def ix_event(d):
        arrived(rows[0].at[rslot(d, False)], ("ix", d))

    P_RECV, P_SEND = ids(recv_ids, ("tp",), 16), ids(send_ids, ("tp",), 8)
    Z_RECV, Z_SEND = ids(recv_ids, ("tz",), 8), ids(send_ids, ("tz",), 16)
    F_RECV, F_SEND = ids(recv_ids, ("tf",), 8), ids(send_ids, ("tf",), 8)

    def cut(k):
        return pl.ds(pl.multiple_of(k * PIECE, PIECE), PIECE)

    def own_tile(t):
        return cols[0].at[r] if t == 0 else rows[0].at[c]

    def p_copy(t, dk):
        k = lax.rem(y + dk, 4)
        return copy(own_tile(t).at[:, cut(k)], stage_p.at[t, r // 2], (4 * k + 2 * lax.rem(z, 2) + x_lo, 2 * z + core),
                    P_SEND + 4 * t + dk, P_RECV + 8 * t + r // 2)

    def p_start(t):
        for dk in (1, 3, 2):
            p_copy(t, dk).start()

        @pl.when(at_home)
        def _():
            stage_p[t, r // 2] = own_tile(t)[:, cut(y)]

        @pl.when(jnp.logical_not(at_home))
        def _():
            p_copy(t, 0).start()

    def z_copy(t, d):
        to = lax.rem(z + d + 8, 8)
        return to, copy(stage_p.at[t, to], stage_z.at[t, z // 2], (r, 2 * to + x_lo), Z_SEND + 8 * t + (d + 8) % 8, Z_RECV + 4 * t + z // 2)

    def z_start(t, ds):
        @pl.when(relay)
        def _():
            for d in ds:
                to, op = z_copy(t, d)

                @pl.when(jnp.logical_not(at_home & (to == r // 2)))
                def _():
                    wait_at(stage_p.at[t, to], P_RECV + 8 * t + to)

                if d:
                    op.start()
                else:
                    stage_z[t, z // 2] = stage_p[t, z]

    def f_copy(t, dz):
        part = lax.rem(y + dz, 4)
        dst = rows[1].at[c, :, cut(y)] if t == 0 else cols[1].at[4 * part + 2 * x_hi + core, :, cut(y)]
        return part, dst, copy(stage_z.at[t, part], dst, (4 * part + 2 * x_hi + core, c), F_SEND + 4 * t + dz, F_RECV + 4 * t + y)

    def f_start(t):
        for dz in (0, 1, 3, 2):
            part, dst, op = f_copy(t, dz)

            @pl.when(jnp.logical_not(relay & (part == z // 2)))
            def _():
                wait_at(stage_z.at[t, part], Z_RECV + 4 * t + part)

            if dz:
                op.start()
            else:
                dst[...] = stage_z[t, part]

    def f_arrived(t):
        for dk in (1, 3, 2):
            k = lax.rem(y + dk, 4)
            wait_at(rows[1].at[c, :, cut(k)] if t == 0 else cols[1].at[r, :, cut(k)], F_RECV + 4 * t + k)

    def exchange_sent():
        for t in (0, 1):
            for dk in (1, 2, 3):
                p_copy(t, dk).wait_send()
                f_copy(t, dk)[2].wait_send()

            @pl.when(jnp.logical_not(at_home))
            def _():
                p_copy(t, 0).wait_send()

            @pl.when(relay)
            def _():
                for d in range(1, 8):
                    z_copy(t, d)[1].wait_send()

    tile = 256
    target = (ladder, partner)

    def term(t, ds, m):
        span = pl.ds(pl.multiple_of(m * tile, tile), tile)
        blocks = [2 * lax.rem(z + d + 8, 8) for d in ds]
        left = jnp.concatenate([rows[t][pl.ds(b, 2), :, span].reshape(192, tile) for b in blocks], 0)
        right = jnp.concatenate([cols[t][pl.ds(b, 2)].reshape(192, 1536) for b in blocks], 0)
        return lax.dot_general(left, right, (((0,), (0,)), ((), ())), preferred_element_type=jnp.float32)

    def product(t, ds, lo, hi, first):
        dest = target[t]

        @pl.loop(lo, hi)
        def _(m):
            span = pl.ds(pl.multiple_of(m * tile, tile), tile)
            if first:
                dest[span, :] = term(t, ds, m)
            else:
                dest[span, :] = dest[span, :] + term(t, ds, m)

    NEAR, MID, LAST = (0, -1, 1, -2), (2, -3, 3), (4,)

    load_i = pltpu.make_async_copy(i_ref, rows0.at[c], load_sems.at[0])
    load_a = pltpu.make_async_copy(a_ref, cols0.at[r], load_sems.at[1])
    load_i.start()
    load_a.start()
    barrier = pltpu.get_barrier_semaphore()

    def greet(device):
        pl.semaphore_signal(barrier, inc=1, device_id=device, device_id_type=MESH)

    for device in (to_x, to_zp, to_zm, to_h, to_yp, to_ym, to_y2, to_core):
        greet(device)

    @pl.when(relay)
    def _():
        for k in range(8):
            @pl.when(jnp.logical_not(at_home & (r // 2 == k)))
            def _():
                greet((2 * k + x_lo, 2 * z + core))

    for k in range(4):
        @pl.when(z != 2 * k + x_hi)
        def _():
            greet((r, 4 * k + 2 * x_hi + x_lo))

    load_i.wait()
    load_a.wait()

    @pl.when(jnp.logical_not(relay))
    def _():
        pl.semaphore_wait(barrier, 12)

    @pl.when(relay & jnp.logical_not(at_home))
    def _():
        pl.semaphore_wait(barrier, 19)

    @pl.when(at_home)
    def _():
        pl.semaphore_wait(barrier, 18)

    ORDER = (0, -1, 1, -2, 2, -3, 3, 4)
    events = [
        (0, lambda: p_start(0)), (0.1, lambda: i_event(0)), (0.2, lambda: p_start(1)), (0.3, lambda: ix_start(0)),
        (0.4, lambda: c_event(0, 0)),
        (9, lambda: z_start(0, ORDER)),
        (11, lambda: i_event(-1)), (11.1, lambda: i_event(1)), (11.2, lambda: ix_start(-1)), (11.3, lambda: ix_start(1)),
        (14, lambda: z_start(1, ORDER)),
        (16, lambda: f_start(0)),
        (25, lambda: c_event(0, 1)), (18.1, lambda: c_event(0, 2)), (18.2, lambda: c_event(0, 3)),
        (19, lambda: i_event(-2)), (19.1, lambda: i_event(2)), (21.2, lambda: ix_start(-2)), (21.3, lambda: ix_start(2)),
        (21, lambda: f_arrived(0)), (21.05, lambda: a_event(0)),
        (23, lambda: f_start(1)),
        (33.3, lambda: c_event(0, 4)), (33.4, lambda: c_event(0, 5)),
        (27, lambda: i_event(-3)), (27.1, lambda: i_event(3)),
        (28, lambda: a_event(1)), (28.1, lambda: ix_start(-3)), (28.2, lambda: ix_start(3)),
        (29, lambda: f_arrived(1)), (29.1, lambda: c_event(1, 0)),
        (33, lambda: i_event(4)), (33.1, lambda: ix_start(4)), (30, lambda: c_event(0, 6)), (43.5, lambda: c_event(0, 7)),
        (36, lambda: a_event(2)), (36.1, lambda: a_event(3)), (52.5, lambda: c_event(1, 1)),
        (42, lambda: a_event(4)), (42.1, lambda: a_event(5)), (43, lambda: c_event(1, 2)), (43.1, lambda: c_event(1, 3)),
        (49, lambda: a_event(6)), (49.1, lambda: a_event(7)), (58.5, lambda: c_event(1, 4)), (58.6, lambda: c_event(1, 5)),
        (55, lambda: a_event(8)), (55.1, lambda: a_event(9)), (50, lambda: c_event(1, 6)), (63, lambda: c_event(1, 7)),
        (61, lambda: a_event(10)), (61.1, lambda: a_event(11)),
        (68, lambda: a_event(12)), (68.1, lambda: a_event(13)),
        (75, lambda: a_event(14)), (76, lambda: a_event(15)),
    ]
    for n in range(8):
        events.append((44, lambda n=n: core_event(0, n)))
        events.append((64, lambda n=n: core_event(1, n)))
    for d in NEAR:
        events.append((44, lambda d=d: ix_event(d)))
    for d in MID + LAST:
        events.append((57, lambda d=d: ix_event(d)))
    for m in range(6):
        events.append(((45, 46, 47, 50, 52, 53)[m], lambda m=m: product(0, NEAR, m, m + 1, True)))
        events.append(((57.5, 59, 60, 62, 63, 64)[m], lambda m=m: product(0, MID + LAST, m, m + 1, False)))
    events.append((65, lambda: product(1, NEAR, 0, 3, True)))
    events.append((69, lambda: product(1, NEAR, 3, 6, True)))
    events.append((70, lambda: product(1, MID, 0, 6, False)))
    for _, event in sorted(events, key=lambda item: item[0]):
        event()
    for op in plain:
        op.wait_send()
    far_copy(1).wait_send()
    exchange_sent()


def finish_kernel(ladder, partner, rows1, cols1, energies, out_ref, buffer, sems):
    r, c = lax.axis_index("row"), lax.axis_index("col")
    last = 2 * lax.rem(c // 2 + 4, 8)
    tile, slots, wide = buffer.shape[1], buffer.shape[0], 512
    size = ladder.shape[0]
    steps = size // tile
    per = size // 128

    def put(m, slot):
        return pltpu.make_async_copy(
            buffer.at[slot], out_ref.at[pl.ds(pl.multiple_of(m * tile, tile), tile), :], sems.at[slot])

    @pl.loop(0, steps)
    def _(m):
        slot = lax.rem(m, slots)

        @pl.when(m >= slots)
        def _():
            put(m - slots, slot).wait()

        span = pl.ds(pl.multiple_of(m * tile, tile), tile)
        left = rows1[pl.ds(last, 2), :, span].reshape(192, tile)
        row_e = jnp.broadcast_to(energies[pl.ds(r * per + m, 1), :], (128, 128)).T
        for n in range(size // wide):
            there = slice(n * wide, (n + 1) * wide)
            right = cols1[pl.ds(last, 2), :, there].reshape(192, wide)
            term = lax.dot_general(left, right, (((0,), (0,)), ((), ())), preferred_element_type=jnp.float32)
            half = (partner[span, there] + term).astype(jnp.bfloat16).astype(jnp.float32)
            total = ladder[span, there] + half
            for j in range(wide // 128):
                denom = row_e + energies[pl.ds(c * per + n * (wide // 128) + j, 1), :]
                inverse = pl.reciprocal(denom, approx=True)
                inverse = inverse * (2.0 - denom * inverse)
                at = n * wide + j * 128
                buffer[slot, :, at:at + 128] = total[:, j * 128:(j + 1) * 128] * inverse
        put(m, slot).start()

    for m in range(steps - slots, steps):
        put(m, m % slots).wait()


def body(integrals, amplitudes, energies):
    size = integrals.shape[0]
    depth = amplitudes.shape[0]
    n = lax.axis_size("col")
    panel = jax.ShapeDtypeStruct((n, depth, size), jnp.bfloat16)
    block = jax.ShapeDtypeStruct((size, size), jnp.float32)
    ladder, partner, rows1, cols1 = pl.pallas_call(
        gather_kernel,
        out_shape=(block, block, panel, panel),
        in_specs=[pl.BlockSpec(memory_space=pltpu.HBM)] * 2,
        out_specs=(pl.BlockSpec(memory_space=pltpu.VMEM),) * 4,
        scratch_shapes=[
            pltpu.VMEM((n, depth, size), jnp.bfloat16),
            pltpu.VMEM((n, depth, size), jnp.bfloat16),
            pltpu.VMEM((2, 8, depth, PIECE), jnp.bfloat16),
            pltpu.VMEM((2, 4, depth, PIECE), jnp.bfloat16),
            pltpu.SemaphoreType.DMA((2,)),
            pltpu.SemaphoreType.DMA((N_SEND,)),
            pltpu.SemaphoreType.DMA((N_RECV,)),
        ],
        compiler_params=pltpu.CompilerParams(
            collective_id=0, has_side_effects=True, vmem_limit_bytes=25_000_000),
    )(integrals.T, amplitudes)
    return pl.pallas_call(
        finish_kernel,
        out_shape=block,
        in_specs=[pl.BlockSpec(memory_space=pltpu.VMEM)] * 5,
        out_specs=pl.BlockSpec(memory_space=pl.ANY),
        scratch_shapes=[
            pltpu.VMEM((3, 128, size), jnp.float32),
            pltpu.SemaphoreType.DMA((3,)),
        ],
        compiler_params=pltpu.CompilerParams(vmem_limit_bytes=16 * MIB),
    )(ladder, partner, rows1, cols1, energies.reshape(-1, 128))


def solution(mesh):
    return jax.shard_map(
        body,
        mesh=mesh,
        in_specs=(P("row", "col"), P("row", "col"), P()),
        out_specs=P("row", "col"),
        check_vma=False,
    )
```
